768 devices in a mesh: grp: 12 (over z), loc: 64 (over x, y, core).
Axes of the slice: x: 4, y: 8, z: 12, core: 2. Of those that a mesh axis runs over, the one named last changes fastest.
Arguments:
- table: float32 [196608, 512], P(('grp', 'loc')), may hold values from -6 to 6
- projection_weight: bfloat16 [512, 2048], replicated, may hold values from -0.25 to 0.25
- output_weight: bfloat16 [512, 512], replicated, may hold values from -0.25 to 0.25
- offsets: int32 [768, 768, 2], P(('grp', 'loc')), may hold values from 0 to 255, as said below
- events: int32 [1536, 176], P(('grp', 'loc')), may hold values from 0 to 1535, as said below
- cotangent: bfloat16 [1536, 176, 512], P(('grp', 'loc')), may hold values from -6 to 6
Outputs:
- layer_out: bfloat16 [1536, 176, 512], P(('grp', 'loc'))
- table_grad: float32 [196608, 512], P(('grp', 'loc'))
The draws below stay inside these ranges and needn't reach their ends.
Inputs may be any that keep to these rules, and one draw needn't show every extreme that they name: Within one device's block for one owner, the 2 offsets differ. For each device, exactly 96 owners have 2 live slots and 144 have 1 live slot (slot c of owner o is live if c is below that owner's count); owners 0 and 767 always have 2 live slots; events name only live slots o * 2 + c of the device's own list, and every live slot is named by at least one event of the device.
All inputs are finite; a program needn't handle non-finite values.
Results may differ from the reference program's by a relative error of at most 0.015.
Values may be sent and summed in bfloat16 or wider, within the bound.
A program may use at most 32 MiB of HBM per device.

```python
import jax
import jax.numpy as jnp
from jax import lax

D = 512
HEADS = 4
SEQS = 2
LEN = 176
ROWS_DEV = 256
CAP = 2
ROWS = 196608
HIST = 1536
DEVICES = 768


def draw_offsets(key, part):
    key = jax.random.fold_in(key, 11)
    key_first, key_step = jax.random.split(key, 2)
    first = jax.random.randint(key_first, (DEVICES, DEVICES), 0, ROWS_DEV)
    offset_step = jax.random.randint(key_step, (DEVICES, DEVICES), 1, ROWS_DEV)
    second = (first + offset_step) % ROWS_DEV
    return jnp.stack([first, second], axis=-1).astype(jnp.int32)


def draw_events(key, part):
    key = jax.random.fold_in(key, 23)
    double_count = DEVICES // 8
    single_count = DEVICES // 8 + DEVICES // 16
    total_live = 2 * double_count + single_count

    def per_device(device_index):
        device_key = jax.random.fold_in(key, device_index)
        key_owner, key_token, key_extra = jax.random.split(device_key, 3)
        middle = jax.random.permutation(key_owner, DEVICES - 2)
        middle_rank = jnp.argsort(middle).astype(jnp.int32) + 2
        owner_rank = jnp.concatenate([jnp.zeros((1,), jnp.int32), middle_rank, jnp.ones((1,), jnp.int32)])
        counts = jnp.where(owner_rank < double_count, 2, jnp.where(owner_rank < double_count + single_count, 1, 0))
        live_slots = (jnp.arange(CAP)[None, :] < counts[:, None]).astype(jnp.int32).reshape(-1)
        running = jnp.cumsum(live_slots)
        token_order = jax.random.permutation(key_token, SEQS * LEN)
        extra_pick = jax.random.randint(key_extra, (SEQS * LEN,), 0, total_live)
        chosen = jnp.where(token_order < total_live, token_order, extra_pick)
        slot_index = jnp.searchsorted(running, chosen + 1, side='left')
        return slot_index.astype(jnp.int32).reshape(SEQS, LEN)
    drawn = jax.vmap(per_device)(jnp.arange(DEVICES))
    return drawn.reshape(DEVICES * SEQS, LEN).astype(jnp.int32)


def block_levels(rng, extent, cuts, least, high):
    level = 1.0
    for axis_at, blocks in cuts:
        heights = jax.random.uniform(jax.random.fold_in(jax.random.fold_in(rng, 6), axis_at), (blocks,), jnp.float32, least / len(cuts), high / len(cuts))
        level = level * jnp.repeat(jnp.exp(heights), extent[axis_at] // blocks).reshape((-1,) + (1,) * (len(extent) - 1 - axis_at))
    return level


def bell_draw(stream_key, extent, deviation, reach, pieces=(), kind=jnp.bfloat16):
    array = deviation * jax.random.normal(stream_key, extent, jnp.float32)
    if pieces:
        array = array * block_levels(stream_key, extent, pieces, -0.22, 0.18)
    return jnp.clip(array, -reach, reach).astype(kind)


def setup_inputs(seed: int = 0) -> dict:
    splits = jax.random.split(jax.random.key(seed), 7)
    return {
        "table": bell_draw(splits[0], (ROWS, D), 1.0, 6.0, ((0, 768),), jnp.float32),
        "projection_weight": bell_draw(splits[1], (D, 4 * D), D ** -0.5, 0.25),
        "output_weight": bell_draw(splits[2], (D, D), D ** -0.5, 0.25),
        "offsets": draw_offsets(jax.random.fold_in(splits[6], 71), 0),
        "events": draw_events(jax.random.fold_in(splits[6], 71), 0),
        "cotangent": bell_draw(splits[5], (HIST, LEN, D), 1.0, 6.0, ((0, 768),)),
    }


def normalize(values):
    center = values - lax.optimization_barrier(jnp.mean(values, axis=-1, keepdims=True))
    spread = lax.optimization_barrier(jnp.mean(center * center, axis=-1, keepdims=True))
    return center * lax.rsqrt(spread + 1e-05)

def hstu_layer(input_rows, projection_weight, output_weight):
    width = input_rows.shape[-1]
    length = input_rows.shape[1]
    normed_rows = normalize(input_rows).astype(jnp.bfloat16)
    branch_parts = jax.nn.silu(jnp.einsum('riq,qu->riu', normed_rows.astype(jnp.float32), projection_weight.astype(jnp.float32)))
    upper = branch_parts[..., :width].astype(jnp.bfloat16)
    values = branch_parts[..., width:2 * width].astype(jnp.bfloat16)
    queries = branch_parts[..., 2 * width:3 * width].astype(jnp.bfloat16)
    keyset = branch_parts[..., 3 * width:].astype(jnp.bfloat16)
    head_dim = width // HEADS
    shape4 = (input_rows.shape[0], length, HEADS, head_dim)
    scores = jnp.einsum('sihd,sjhd->shij', queries.reshape(shape4).astype(jnp.float32), keyset.reshape(shape4).astype(jnp.float32))
    scores = scores * (1.0 / head_dim ** 0.5)
    causal = jnp.arange(length)[:, None] >= jnp.arange(length)[None, :]
    weights = jnp.where(causal, jax.nn.silu(scores) / LEN, 0.0).astype(jnp.bfloat16)
    attended = jnp.einsum('shij,sjhd->sihd', weights.astype(jnp.float32), values.reshape(shape4).astype(jnp.float32))
    attended = attended.reshape(input_rows.shape)
    gated_values = (normalize(attended) * upper.astype(jnp.float32)).astype(jnp.bfloat16)
    return input_rows + jnp.einsum('riq,qu->riu', gated_values.astype(jnp.float32), output_weight.astype(jnp.float32))

def reference(table, projection_weight, output_weight, offsets, events, cotangent):

    def requester_step(grad_total, items):
        offset_rows, event_row_block, cot_rows = items
        owners = jnp.arange(DEVICES, dtype=jnp.int32)[:, None] * ROWS_DEV
        row_ids = (owners + offset_rows).reshape(-1).astype(jnp.int32)
        fetched = lax.optimization_barrier(table[row_ids].astype(jnp.bfloat16))
        input_rows = fetched[event_row_block].astype(jnp.float32)
        output, pullback = jax.vjp(lambda given: hstu_layer(given, projection_weight, output_weight), input_rows)
        input_grad = pullback(cot_rows.astype(jnp.float32))[0]
        slot_grad = jnp.zeros((DEVICES * CAP, D), jnp.float32).at[event_row_block.reshape(-1)].add(input_grad.reshape(-1, D))
        rounded = lax.optimization_barrier(slot_grad.astype(jnp.bfloat16)).astype(jnp.float32)
        grad_total = grad_total.at[row_ids].add(rounded)
        return (grad_total, output.astype(jnp.bfloat16))
    start = jnp.zeros((ROWS_DEV * DEVICES, D), jnp.float32)
    table_grad, outputs = lax.scan(requester_step, start, (offsets, events.reshape(DEVICES, SEQS, LEN), cotangent.reshape(DEVICES, SEQS, LEN, D)))
    return (outputs.reshape(DEVICES * SEQS, LEN, D), table_grad)
```

```python
import functools

import jax
import jax.numpy as jnp
from jax import lax
from jax.experimental import pallas as pl
from jax.experimental.pallas import tpu as pltpu
from jax.sharding import PartitionSpec as P

MESH = pl.DeviceIdType.MESH
F32, BF16 = jnp.float32, jnp.bfloat16
GROUPS, LOCS, CHIPS = 12, 64, 32
ROWS, WIDTH, HEADS, LEN, SEQS = 256, 512, 4, 176, 2
EVENTS = SEQS * LEN
HEAD = WIDTH // HEADS
ORDER = (0, 1, -1, 2, -2, 3, -3, 4, -4, 5, -5, 6)
CHUNKS, PER = 3, 4
MSG = PER * 4
SLOTS = CHIPS * MSG
HALF = ROWS // 2


def place(k):
    return ORDER.index(6 if k == -6 else k)


def parts(hop, side):
    return (0, 1) if hop < 5 else ((0,) if side == 0 else (1,))


def dot(a, b, ca=1, cb=0):
    return lax.dot_general(a, b, (((ca,), (cb,)), ((), ())), preferred_element_type=F32)


def hot(mask):
    return jnp.where(mask, 1.0, 0.0).astype(BF16)


def iota(shape, dim):
    return lax.broadcasted_iota(jnp.int32, shape, dim)


def event_slot(ev, g):
    k = (ev >> 7) - g
    k = jnp.where(k < 0, k + GROUPS, k)
    at = jnp.where(k == 0, 0, jnp.where(k <= 6, 2 * k - 1, 2 * (GROUPS - k)))
    return (at >> 2) * SLOTS + ((ev & 127) >> 2) * MSG + (at & 3) * 4 + (ev & 3)


def lane_of(row, ch, g):
    which = (row & (MSG - 1)) >> 2
    lane = row & 3
    for j in range(PER):
        there = lax.rem(g + ORDER[PER * ch + j] + GROUPS, GROUPS)
        lane = lane + jnp.where(which == j, 4 * there, 0)
    return lane


def norm_stats(x):
    center = x - jnp.mean(x, axis=-1, keepdims=True)
    rstd = lax.rsqrt(jnp.mean(center * center, axis=-1, keepdims=True) + 1e-05)
    return center * rstd, rstd


def norm_back(grad, normed, rstd):
    m1 = jnp.mean(grad, axis=-1, keepdims=True)
    m2 = jnp.mean(grad * normed, axis=-1, keepdims=True)
    return rstd * (grad - m1 - normed * m2)


def kernel(
    table, req, evc, evr, cot_h, wp_h, wo_h, out, tgrad,
    wp, wo, cot, w_sem,
    ag, rq, sb, fet, sg, ret, own, sx_out, sx_in, rs_out, rs_in,
    xhat_s, dsilu, branch, dbranch, att,
    zs, zr, sib_s, sib_r, q_s, q_r, f_s, f_r, b_s, b_r, sx_s, sx_r, rs_s, rs_r,
):
    g, l = lax.axis_index("grp"), lax.axis_index("loc")
    chip, core = lax.div(l, 2), lax.rem(l, 2)
    sib = l + 1 - 2 * core
    nxt = (lax.rem(g + 1, GROUPS), lax.rem(g + GROUPS - 1, GROUPS))

    loads = [
        pltpu.make_async_copy(a, b, w_sem.at[i])
        for i, (a, b) in enumerate(((wp_h, wp), (wo_h, wo), (cot_h, cot)))
    ]
    for load in loads:
        load.start()

    def remote(src, dst, s, r, who):
        return pltpu.make_async_remote_copy(
            src_ref=src, dst_ref=dst, send_sem=s, recv_sem=r, device_id=who, device_id_type=MESH
        )

    bar = pltpu.get_barrier_semaphore()

    def greet(i, _):
        d = lax.rem(chip + i, CHIPS)
        pl.semaphore_signal(bar, inc=1, device_id=(g, 2 * d + core), device_id_type=MESH)
        return 0

    for to in nxt:
        pl.semaphore_signal(bar, inc=1, device_id=(to, l), device_id_type=MESH)
    pl.semaphore_signal(bar, inc=1, device_id=(g, sib), device_id_type=MESH)
    lax.fori_loop(1, CHIPS, greet, 0)
    ag[0, pl.ds(core, 1)] = table[...].astype(BF16)[None]
    rq[pl.ds(chip, 1)] = req[pl.ds(chip, 1)]
    pl.semaphore_wait(bar, CHIPS + 2)

    def ring(side, hop, p):
        sign = -1 if side == 0 else 1
        a, b = place(sign * hop), place(sign * (hop + 1))
        rows = pl.ds(p * HALF, HALF)
        return remote(
            ag.at[a, core, rows], ag.at[b, core, rows], zs.at[side, hop, p], zr.at[side, hop, p], (nxt[side], l)
        )

    def share(at, p):
        rows = pl.ds(p * HALF, HALF)
        return remote(
            ag.at[at, core, rows], ag.at[at, core, rows], sib_s.at[at, p], sib_r.at[at, p], (g, sib)
        )

    for p in range(2):
        ring(0, 0, p).start()
        ring(1, 0, p).start()

    def ask(i, _):
        d = lax.rem(chip + i, CHIPS)
        remote(req.at[d], rq.at[chip], q_s, q_r, (g, 2 * d + core)).start()
        return 0

    lax.fori_loop(1, CHIPS, ask, 0)
    for p in range(2):
        share(0, p).start()

    def spread(src, dst, s, r):
        def one(i, _):
            d = lax.rem(chip + i, CHIPS)
            remote(src.at[d], dst.at[chip], s, r, (g, 2 * d + core)).start()
            return 0

        lax.fori_loop(1, CHIPS, one, 0)
        dst[pl.ds(chip, 1)] = src[pl.ds(chip, 1)]

    def landed(ref, sem):
        view = ref.at[pl.ds(0, CHIPS - 1)]
        pltpu.make_async_copy(view, view, sem).wait()

    def requests():
        return rq[...].reshape(CHIPS, 128).astype(F32).astype(BF16)

    def answer(ch):
        row = iota((SLOTS, 128), 0)
        spread_rows = hot((iota((SLOTS, CHIPS), 0) >> 4) == iota((SLOTS, CHIPS), 1))
        picked = jnp.where(iota((SLOTS, 128), 1) == lane_of(row, ch, g), dot(spread_rows, requests()), 0.0)
        index = dot(picked.astype(BF16), jnp.ones((128, 128), BF16)).astype(jnp.int32)
        target = index + 256 * ((row & (MSG - 1)) >> 1)
        lane = iota((SLOTS, 128), 1)
        pick = jnp.concatenate([hot(target == lane + 128 * b) for b in range(16)], axis=1)
        block = ag[pl.ds(PER * ch, PER)].reshape(PER * 2 * ROWS, WIDTH)
        sb[ch] = dot(pick, block).astype(BF16).reshape(CHIPS, MSG, WIDTH)
        spread(sb.at[ch], fet.at[ch], f_s.at[ch], f_r.at[ch])

    shared = [0]
    for hop in range(6):
        for p in range(2):
            for side in range(2):
                if p in parts(hop, side):
                    at = place((-1 if side == 0 else 1) * (hop + 1))
                    ring(side, hop, p).wait_recv()
                    if hop < 5 and p in parts(hop + 1, side):
                        ring(side, hop + 1, p).start()
                    share(at, p).start()
        if hop % 2 == 1:
            ch = hop // 2
            if ch == 0:
                landed(req, q_s)
                landed(rq, q_r)
            for at in range(PER * ch, PER * ch + PER):
                for p in range(2):
                    share(at, p).wait_recv()
            answer(ch)

    slot_c = event_slot(evc[...], g)
    slot_r = event_slot(evr[...], g)
    x = jnp.zeros((EVENTS, WIDTH), F32)
    for ch in range(CHUNKS):
        landed(fet.at[ch], f_r.at[ch])
        x += dot(hot(slot_c - SLOTS * ch == iota((EVENTS, SLOTS), 1)), fet[ch].reshape(SLOTS, WIDTH))
    for load in loads:
        load.wait()

    xhat, xrstd = norm_stats(x)
    xhat_s[...] = xhat
    normed = xhat.astype(BF16)
    for b in range(4):
        v = dot(normed, wp[:, b * WIDTH : (b + 1) * WIDTH])
        sig = 1.0 / (1.0 + jnp.exp(-v))
        branch[b] = (v * sig).astype(BF16)
        dsilu[b] = sig * (1.0 + v * (1.0 - sig))
    scale = 1.0 / HEAD**0.5
    causal = iota((LEN, LEN), 0) >= iota((LEN, LEN), 1)

    def head(b, s, h):
        return branch[b, s * LEN : (s + 1) * LEN, h * HEAD : (h + 1) * HEAD]

    def weigh(s, h):
        sc = dot(head(2, s, h), head(3, s, h), 1, 1) * scale
        sig = 1.0 / (1.0 + jnp.exp(-sc))
        return jnp.where(causal, sc * sig / LEN, 0.0).astype(BF16), jnp.where(
            causal, sig * (1.0 + sc * (1.0 - sig)), 0.0
        )

    for s in range(SEQS):
        for h in range(HEADS):
            w, _ = weigh(s, h)
            att[s * LEN : (s + 1) * LEN, h * HEAD : (h + 1) * HEAD] = dot(w, head(1, s, h))
    ahat, arstd = norm_stats(att[...])
    upper = branch[0].astype(F32)
    gated = (ahat * upper).astype(BF16)
    out[...] = (x + dot(gated, wo[...])).astype(BF16)

    dgated = dot(cot[...], wo[...], 1, 1).astype(BF16).astype(F32)
    dbranch[0] = ((dgated * ahat).astype(BF16).astype(F32) * dsilu[0]).astype(BF16)
    att[...] = norm_back(dgated * upper, ahat, arstd)
    for s in range(SEQS):
        for h in range(HEADS):
            rows, cols = slice(s * LEN, (s + 1) * LEN), slice(h * HEAD, (h + 1) * HEAD)
            w, slope = weigh(s, h)
            da = att[rows, cols].astype(BF16)
            dw = dot(da, head(1, s, h), 1, 1).astype(BF16).astype(F32)
            dsc = (dw * slope * (scale / LEN)).astype(BF16)
            for b, val in (
                (1, dot(w, da, 0, 0)),
                (2, dot(dsc, head(3, s, h))),
                (3, dot(dsc, head(2, s, h), 0, 0)),
            ):
                dbranch[b, rows, cols] = (
                    val.astype(BF16).astype(F32) * dsilu[b, rows, cols]
                ).astype(BF16)
    dnormed = jnp.zeros((EVENTS, WIDTH), F32)
    for b in range(4):
        dnormed += dot(dbranch[b], wp[:, b * WIDTH : (b + 1) * WIDTH], 1, 1)
    dx = cot[...].astype(F32) + norm_back(dnormed.astype(BF16).astype(F32), xhat_s[...], xrstd)
    high = dx.astype(BF16)
    low = (dx - high.astype(F32)).astype(BF16)
    for ch in reversed(range(CHUNKS)):
        where = hot(slot_r - SLOTS * ch == iota((SLOTS, EVENTS), 0))
        sg[ch] = (dot(where, high) + dot(where, low)).astype(BF16).reshape(CHIPS, MSG, WIDTH)
        spread(sg.at[ch], ret.at[ch], b_s.at[ch], b_r.at[ch])

    def swap(at):
        return remote(sx_out.at[at], sx_in.at[at], sx_s.at[at], sx_r.at[at], (g, sib))

    def collect(ch):
        landed(ret.at[ch], b_r.at[ch])
        lane, col = iota((128, SLOTS), 0), iota((128, SLOTS), 1)
        sel = dot(requests(), hot(lane == lane_of(col, ch, g)))
        mine = (iota((CHIPS, SLOTS), 1) >> 4) == iota((CHIPS, SLOTS), 0)
        index = dot(jnp.ones((8, CHIPS), BF16), jnp.where(mine, sel, 0.0).astype(BF16))[0:1].astype(jnp.int32)
        kind = (iota((1, SLOTS), 1) & (MSG - 1)) >> 1
        row = iota((ROWS, SLOTS), 0)
        grads = ret[ch].reshape(SLOTS, WIDTH)
        for j in reversed(range(PER)):
            at = PER * ch + j
            for other in (True, False):
                col_core = 1 - core if other else core
                mine = jnp.where(kind == 2 * j + col_core, index, -1)
                total = dot(hot(row == mine), grads)
                if other:
                    sx_out[at] = total.astype(BF16)
                    swap(at).start()
                else:
                    own[at] = total

    def pass_on(side, s, p):
        rows = pl.ds(p * HALF, HALF)
        return remote(
            rs_out.at[side, s - 1, rows], rs_in.at[side, s - 1, rows],
            rs_s.at[side, 6 - s, p], rs_r.at[side, 6 - s, p], (nxt[side], l),
        )

    done, got = [], []
    for s in range(6, -1, -1):
        for side in range(2):
            at = place(s if side == 0 else -s)
            if at // PER not in done:
                collect(at // PER)
                done.append(at // PER)
            if at not in got:
                swap(at).wait_recv()
                got.append(at)
            if s == 0:
                continue
            for p in ((0, 1) if s < 6 else (side,)):
                rows = slice(p * HALF, (p + 1) * HALF)
                total = own[at, rows] + sx_in[at, rows].astype(F32)
                if s < 5 or (s == 5 and p == side):
                    pass_on(side, s + 1, p).wait_recv()
                    total += rs_in[side, s, rows].astype(F32)
                rs_out[side, s - 1, rows] = total.astype(BF16)
                pass_on(side, s, p).start()
    for p in range(2):
        rows = slice(p * HALF, (p + 1) * HALF)
        total = own[0, rows] + sx_in[0, rows].astype(F32)
        for side in range(2):
            pass_on(side, 1, p).wait_recv()
            total += rs_in[side, 0, rows].astype(F32)
        tgrad[rows] = total

    for side in range(2):
        for hop in range(6):
            for p in parts(hop, side):
                ring(side, hop, p).wait_send()
        for s in range(1, 7):
            for p in ((0, 1) if s < 6 else (side,)):
                pass_on(side, s, p).wait_send()
    for at in range(GROUPS):
        for p in range(2):
            share(at, p).wait_send()
        swap(at).wait_send()
    for ch in range(CHUNKS):
        landed(sb.at[ch], f_s.at[ch])
        landed(sg.at[ch], b_s.at[ch])


def local(table, projection_weight, output_weight, offsets, events, cotangent):
    asked = offsets.reshape(GROUPS, CHIPS, 4).transpose(1, 0, 2).reshape(CHIPS, 1, 4 * GROUPS)
    asked = jnp.pad(asked, ((0, 0), (0, 0), (0, 128 - 4 * GROUPS)))
    vmem, anym = pl.BlockSpec(memory_space=pltpu.VMEM), pl.BlockSpec(memory_space=pl.ANY)
    dma = pltpu.SemaphoreType.DMA
    out, grad = pl.pallas_call(
        kernel,
        out_shape=(
            jax.ShapeDtypeStruct((EVENTS, WIDTH), BF16),
            jax.ShapeDtypeStruct((ROWS, WIDTH), F32),
        ),
        in_specs=[vmem] * 4 + [anym] * 3,
        out_specs=(vmem, vmem),
        scratch_shapes=[
            pltpu.VMEM((WIDTH, 4 * WIDTH), BF16),
            pltpu.VMEM((WIDTH, WIDTH), BF16),
            pltpu.VMEM((EVENTS, WIDTH), BF16),
            dma((3,)),
            pltpu.VMEM((GROUPS, 2, ROWS, WIDTH), BF16),
            pltpu.VMEM((CHIPS, 1, 128), jnp.int32),
            pltpu.VMEM((CHUNKS, CHIPS, MSG, WIDTH), BF16),
            pltpu.VMEM((CHUNKS, CHIPS, MSG, WIDTH), BF16),
            pltpu.VMEM((CHUNKS, CHIPS, MSG, WIDTH), BF16),
            pltpu.VMEM((CHUNKS, CHIPS, MSG, WIDTH), BF16),
            pltpu.VMEM((GROUPS, ROWS, WIDTH), F32),
            pltpu.VMEM((GROUPS, ROWS, WIDTH), BF16),
            pltpu.VMEM((GROUPS, ROWS, WIDTH), BF16),
            pltpu.VMEM((2, 6, ROWS, WIDTH), BF16),
            pltpu.VMEM((2, 6, ROWS, WIDTH), BF16),
            pltpu.VMEM((EVENTS, WIDTH), F32),
            pltpu.VMEM((4, EVENTS, WIDTH), F32),
            pltpu.VMEM((4, EVENTS, WIDTH), BF16),
            pltpu.VMEM((4, EVENTS, WIDTH), BF16),
            pltpu.VMEM((EVENTS, WIDTH), F32),
            dma((2, 6, 2)), dma((2, 6, 2)), dma((GROUPS, 2)), dma((GROUPS, 2)),
            dma, dma, dma((CHUNKS,)), dma((CHUNKS,)), dma((CHUNKS,)), dma((CHUNKS,)),
            dma((GROUPS,)), dma((GROUPS,)), dma((2, 6, 2)), dma((2, 6, 2)),
        ],
        compiler_params=pltpu.CompilerParams(
            collective_id=0, has_side_effects=True, vmem_limit_bytes=60 << 20
        ),
    )(
        table,
        asked,
        events.reshape(EVENTS, 1),
        events.reshape(1, EVENTS),
        cotangent.reshape(EVENTS, WIDTH),
        projection_weight,
        output_weight,
    )
    return out.reshape(cotangent.shape), grad


def solution(mesh):
    placed = (
        P(("grp", "loc"), None),
        P(),
        P(),
        P(("grp", "loc"), None, None),
        P(("grp", "loc"), None),
        P(("grp", "loc"), None, None),
    )
    return jax.shard_map(
        local,
        mesh=mesh,
        in_specs=placed,
        out_specs=(P(("grp", "loc"), None, None), P(("grp", "loc"), None)),
        check_vma=False,
    )
```

```python
import functools

import jax
import jax.numpy as jnp
from jax import lax
from jax.experimental import pallas as pl
from jax.experimental.pallas import tpu as pltpu
from jax.sharding import PartitionSpec as P

MESH = pl.DeviceIdType.MESH
F32, BF16 = jnp.float32, jnp.bfloat16
GROUPS, LOCS, CHIPS = 12, 64, 32
ROWS, WIDTH, HEADS, LEN, SEQS = 256, 512, 4, 176, 2
EVENTS = SEQS * LEN
HEAD = WIDTH // HEADS
ORDER = (0, 1, -1, 2, -2, 3, -3, 4, -4, 5, -5, 6)
CHUNKS, PER = 6, 2
MSG = PER * 4
SLOTS = CHIPS * MSG
SIDE = WIDTH // 2
HALF = ROWS // 2


def place(k):
    return ORDER.index(6 if k == -6 else k)


def parts(hop, side):
    return (0, 1) if hop < 5 else ((0,) if side == 0 else (1,))


def dot(a, b, ca=1, cb=0):
    return lax.dot_general(a, b, (((ca,), (cb,)), ((), ())), preferred_element_type=F32)


def hot(mask):
    return jnp.where(mask, 1.0, 0.0).astype(BF16)


def iota(shape, dim):
    return lax.broadcasted_iota(jnp.int32, shape, dim)


def event_slot(ev, g):
    k = (ev >> 7) - g
    k = jnp.where(k < 0, k + GROUPS, k)
    at = jnp.where(k == 0, 0, jnp.where(k <= 6, 2 * k - 1, 2 * (GROUPS - k)))
    return (at >> 1) * SLOTS + ((ev & 127) >> 2) * MSG + (at & 1) * 4 + (ev & 3)


def lane_of(row, ch, g):
    which = (row & (MSG - 1)) >> 2
    lane = row & 3
    for j in range(PER):
        there = lax.rem(g + ORDER[PER * ch + j] + GROUPS, GROUPS)
        lane = lane + jnp.where(which == j, 4 * there, 0)
    return lane


def stack(x):
    x = x.astype(BF16).astype(F32).reshape(CHIPS, MSG, WIDTH)
    return jnp.concatenate([x[:, :, :SIDE], x[:, :, SIDE:]], axis=1).astype(BF16)


def unstack(x):
    x = x.astype(F32)
    x = jnp.concatenate([x[:, :MSG], x[:, MSG:]], axis=2)
    return x.reshape(SLOTS, WIDTH).astype(BF16)


def norm_stats(x):
    center = x - jnp.mean(x, axis=-1, keepdims=True)
    rstd = lax.rsqrt(jnp.mean(center * center, axis=-1, keepdims=True) + 1e-05)
    return center * rstd, rstd


def norm_back(grad, normed, rstd):
    m1 = jnp.mean(grad, axis=-1, keepdims=True)
    m2 = jnp.mean(grad * normed, axis=-1, keepdims=True)
    return rstd * (grad - m1 - normed * m2)


def kernel(
    table_h, offs, evs, cot_h, wp_h, wo_h, out, tgrad,
    table, wp, wo, cot, w_sem,
    ag, req, rq, sb, fet, sg, ret, own, sx_out, sx_in, rs_out, rs_in,
    xhat_s, dsilu, branch, dbranch, att,
    zs, zr, sib_s, sib_r, q_s, q_r, f_s, f_r, b_s, b_r, sx_s, sx_r, rs_s, rs_r,
):
    g, l = lax.axis_index("grp"), lax.axis_index("loc")
    chip, core = lax.div(l, 2), lax.rem(l, 2)
    sib = l + 1 - 2 * core
    nxt = (lax.rem(g + 1, GROUPS), lax.rem(g + GROUPS - 1, GROUPS))

    loads = [
        pltpu.make_async_copy(a, b, w_sem.at[i])
        for i, (a, b) in enumerate(((table_h, table), (wp_h, wp), (wo_h, wo), (cot_h, cot)))
    ]
    for load in loads:
        load.start()

    def remote(src, dst, s, r, who):
        return pltpu.make_async_remote_copy(
            src_ref=src, dst_ref=dst, send_sem=s, recv_sem=r, device_id=who, device_id_type=MESH
        )

    bar = pltpu.get_barrier_semaphore()

    def greet(i, _):
        d = lax.rem(chip + i, CHIPS)
        pl.semaphore_signal(bar, inc=1, device_id=(g, 2 * d + core), device_id_type=MESH)
        return 0

    for to in nxt:
        pl.semaphore_signal(bar, inc=1, device_id=(to, l), device_id_type=MESH)
    pl.semaphore_signal(bar, inc=1, device_id=(g, sib), device_id_type=MESH)
    lax.fori_loop(1, CHIPS, greet, 0)
    owner, lane = iota((WIDTH + SIDE, 128), 0), iota((WIDTH + SIDE, 128), 1)
    asks = jnp.zeros((CHIPS, 128), F32)
    of_chip = (iota((CHIPS, WIDTH + SIDE), 1) & (LOCS - 1)) >> 1 == iota((CHIPS, WIDTH + SIDE), 0)
    for slot in range(2):
        picked = jnp.where(of_chip, offs[slot : slot + 1].astype(F32), 0.0).astype(BF16)
        asks += dot(picked, hot(lane == (owner >> 6) * 4 + (owner & 1) * 2 + slot))
    req[...] = asks.reshape(CHIPS, 1, 128)
    loads[0].wait()
    ag[0, pl.ds(core, 1)] = table[...].astype(BF16)[None]
    rq[pl.ds(chip, 1)] = req[pl.ds(chip, 1)]
    pl.semaphore_wait(bar, CHIPS + 2)

    def ring(side, hop, p):
        sign = -1 if side == 0 else 1
        a, b = place(sign * hop), place(sign * (hop + 1))
        rows = pl.ds(p * HALF, HALF)
        return remote(
            ag.at[a, core, rows], ag.at[b, core, rows], zs.at[side, hop, p], zr.at[side, hop, p], (nxt[side], l)
        )

    def share(at, p):
        rows = pl.ds(p * HALF, HALF)
        return remote(
            ag.at[at, core, rows], ag.at[at, core, rows], sib_s.at[at, p], sib_r.at[at, p], (g, sib)
        )

    for p in range(2):
        ring(0, 0, p).start()
        ring(1, 0, p).start()

    def ask(i, _):
        d = lax.rem(chip + i, CHIPS)
        remote(req.at[d], rq.at[chip], q_s, q_r, (g, 2 * d + core)).start()
        return 0

    lax.fori_loop(1, CHIPS, ask, 0)
    for p in range(2):
        share(0, p).start()

    def spread(src, dst, s, r, first=1, last=CHIPS):
        def one(i, _):
            d = lax.rem(chip + i, CHIPS)
            remote(src.at[d], dst.at[chip], s, r, (g, 2 * d + core)).start()
            return 0

        lax.fori_loop(first, last, one, 0)
        if last == CHIPS:
            dst[pl.ds(chip, 1)] = src[pl.ds(chip, 1)]

    def landed(ref, sem):
        view = ref.at[pl.ds(0, CHIPS - 1)]
        pltpu.make_async_copy(view, view, sem).wait()

    def requests():
        return rq[...].reshape(CHIPS, 128).astype(BF16)

    def answer(ch):
        row = iota((SLOTS, 128), 0)
        spread_rows = hot((iota((SLOTS, CHIPS), 0) >> 3) == iota((SLOTS, CHIPS), 1))
        picked = jnp.where(iota((SLOTS, 128), 1) == lane_of(row, ch, g), dot(spread_rows, requests()), 0.0)
        index = dot(picked.astype(BF16), jnp.ones((128, 128), BF16)).astype(jnp.int32)
        target = index + 256 * ((row & (MSG - 1)) >> 1)
        lane = iota((SLOTS, 128), 1)
        pick = jnp.concatenate([hot(target == lane + 128 * b) for b in range(4 * PER)], axis=1)
        block = ag[pl.ds(PER * ch, PER)].reshape(PER * 2 * ROWS, WIDTH)
        sb[ch] = stack(dot(pick, block))

    def send_answer(ch, first, last):
        spread(sb.at[ch], fet.at[ch], f_s.at[ch], f_r.at[ch], first, last)

    def shares_landed(ch):
        for at in range(PER * ch, PER * ch + PER):
            for p in range(2):
                share(at, p).wait_recv()

    for hop in range(6):
        for p in range(2):
            for side in range(2):
                if p in parts(hop, side):
                    at = place((-1 if side == 0 else 1) * (hop + 1))
                    ring(side, hop, p).wait_recv()
                    if hop < 5 and p in parts(hop + 1, side):
                        ring(side, hop + 1, p).start()
                    share(at, p).start()
            if hop and p == 0:
                shares_landed(hop - 1)
                answer(hop - 1)
                send_answer(hop - 1, 1, CHIPS // 2)
            elif hop:
                send_answer(hop - 1, CHIPS // 2, CHIPS)
            elif p:
                landed(req, q_s)
                landed(rq, q_r)
    shares_landed(5)
    answer(5)
    send_answer(5, 1, CHIPS)

    slot_r = event_slot(evs[...], g)
    slot_c = []
    for s in range(SEQS):
        digits = jnp.where(iota((16, LEN), 0) == 0, slot_r[s : s + 1] >> 8, 0)
        digits = jnp.where(iota((16, LEN), 0) == 1, slot_r[s : s + 1] & 255, digits)
        worth = jnp.where(iota((16, 128), 0) == 0, 256.0, 1.0).astype(BF16)
        slot_c.append(dot(digits.astype(F32).astype(BF16), worth, 0, 0).astype(jnp.int32))
    slot_c = jnp.concatenate(slot_c, axis=0)
    x = jnp.zeros((EVENTS, WIDTH), F32)
    for ch in range(CHUNKS):
        landed(fet.at[ch], f_r.at[ch])
        where = [hot(slot_c - SLOTS * ch - 128 * b == iota((EVENTS, 128), 1)) for b in range(SLOTS // 128)]
        x += dot(jnp.concatenate(where, axis=1), unstack(fet[ch]))
    for load in loads[1:]:
        load.wait()

    xhat, xrstd = norm_stats(x)
    xhat_s[...] = xhat
    normed = xhat.astype(BF16)
    for b in range(4):
        v = dot(normed, wp[:, b * WIDTH : (b + 1) * WIDTH])
        sig = 1.0 / (1.0 + jnp.exp(-v))
        branch[b] = (v * sig).astype(BF16)
        dsilu[b] = sig * (1.0 + v * (1.0 - sig))
    scale = 1.0 / HEAD**0.5
    causal = iota((LEN, LEN), 0) >= iota((LEN, LEN), 1)

    def head(b, s, h):
        return branch[b, s * LEN : (s + 1) * LEN, h * HEAD : (h + 1) * HEAD]

    def weigh(s, h):
        sc = dot(head(2, s, h), head(3, s, h), 1, 1) * scale
        sig = 1.0 / (1.0 + jnp.exp(-sc))
        return jnp.where(causal, sc * sig / LEN, 0.0).astype(BF16), jnp.where(
            causal, sig * (1.0 + sc * (1.0 - sig)), 0.0
        )

    for s in range(SEQS):
        for h in range(HEADS):
            w, _ = weigh(s, h)
            att[s * LEN : (s + 1) * LEN, h * HEAD : (h + 1) * HEAD] = dot(w, head(1, s, h))
    ahat, arstd = norm_stats(att[...])
    upper = branch[0].astype(F32)
    gated = (ahat * upper).astype(BF16)
    out[...] = (x + dot(gated, wo[...])).astype(BF16)

    dgated = dot(cot[...], wo[...], 1, 1).astype(BF16).astype(F32)
    dbranch[0] = ((dgated * ahat).astype(BF16).astype(F32) * dsilu[0]).astype(BF16)
    att[...] = norm_back(dgated * upper, ahat, arstd)
    for s in range(SEQS):
        for h in range(HEADS):
            rows, cols = slice(s * LEN, (s + 1) * LEN), slice(h * HEAD, (h + 1) * HEAD)
            w, slope = weigh(s, h)
            da = att[rows, cols].astype(BF16)
            dw = dot(da, head(1, s, h), 1, 1).astype(BF16).astype(F32)
            dsc = (dw * slope * (scale / LEN)).astype(BF16)
            for b, val in (
                (1, dot(w, da, 0, 0)),
                (2, dot(dsc, head(3, s, h))),
                (3, dot(dsc, head(2, s, h), 0, 0)),
            ):
                dbranch[b, rows, cols] = (
                    val.astype(BF16).astype(F32) * dsilu[b, rows, cols]
                ).astype(BF16)
    dnormed = jnp.zeros((EVENTS, WIDTH), F32)
    for b in range(4):
        dnormed += dot(dbranch[b], wp[:, b * WIDTH : (b + 1) * WIDTH], 1, 1)
    dx = cot[...].astype(F32) + norm_back(dnormed.astype(BF16).astype(F32), xhat_s[...], xrstd)
    high = dx.astype(BF16)
    low = (dx - high.astype(F32)).astype(BF16)

    def send_grads(ch):
        total = jnp.zeros((SLOTS, WIDTH), F32)
        for s in range(SEQS):
            where = hot(slot_r[s : s + 1] - SLOTS * ch == iota((SLOTS, LEN), 0))
            rows = slice(s * LEN, (s + 1) * LEN)
            total += dot(where, high[rows]) + dot(where, low[rows])
        sg[ch] = stack(total)
        spread(sg.at[ch], ret.at[ch], b_s.at[ch], b_r.at[ch])

    def swap(at):
        return remote(sx_out.at[at], sx_in.at[at], sx_s.at[at], sx_r.at[at], (g, sib))

    def collect(ch):
        landed(ret.at[ch], b_r.at[ch])
        lane, col = iota((128, SLOTS), 0), iota((128, SLOTS), 1)
        sel = dot(requests(), hot(lane == lane_of(col, ch, g)))
        mine = (iota((CHIPS, SLOTS), 1) >> 3) == iota((CHIPS, SLOTS), 0)
        index = dot(jnp.ones((8, CHIPS), BF16), jnp.where(mine, sel, 0.0).astype(BF16))[0:1].astype(jnp.int32)
        kind = (iota((1, SLOTS), 1) & (MSG - 1)) >> 1
        row = iota((ROWS, SLOTS), 0)
        grads = unstack(ret[ch])
        for j in reversed(range(PER)):
            at = PER * ch + j
            for other in (True, False):
                col_core = 1 - core if other else core
                mine = jnp.where(kind == 2 * j + col_core, index, -1)
                total = dot(hot(row == mine), grads)
                if other:
                    sx_out[at] = total.astype(BF16)
                    swap(at).start()
                else:
                    own[at] = total

    def pass_on(side, s, p):
        rows = pl.ds(p * HALF, HALF)
        return remote(
            rs_out.at[side, s - 1, rows], rs_in.at[side, s - 1, rows],
            rs_s.at[side, 6 - s, p], rs_r.at[side, 6 - s, p], (nxt[side], l),
        )

    for ch in reversed(range(CHUNKS)):
        send_grads(ch)
    got = []
    for s in range(6, -1, -1):
        if s:
            collect(s - 1)
        for side in range(2):
            at = place(s if side == 0 else -s)
            if at not in got:
                swap(at).wait_recv()
                got.append(at)
            if s == 0:
                continue
            for p in ((0, 1) if s < 6 else (side,)):
                rows = slice(p * HALF, (p + 1) * HALF)
                total = own[at, rows] + sx_in[at, rows].astype(F32)
                if s < 5 or (s == 5 and p == side):
                    pass_on(side, s + 1, p).wait_recv()
                    total += rs_in[side, s, rows].astype(F32)
                rs_out[side, s - 1, rows] = total.astype(BF16)
                pass_on(side, s, p).start()
    for p in range(2):
        rows = slice(p * HALF, (p + 1) * HALF)
        total = own[0, rows] + sx_in[0, rows].astype(F32)
        for side in range(2):
            pass_on(side, 1, p).wait_recv()
            total += rs_in[side, 0, rows].astype(F32)
        tgrad[rows] = total

    for side in range(2):
        for hop in range(6):
            for p in parts(hop, side):
                ring(side, hop, p).wait_send()
        for s in range(1, 7):
            for p in ((0, 1) if s < 6 else (side,)):
                pass_on(side, s, p).wait_send()
    for at in range(GROUPS):
        for p in range(2):
            share(at, p).wait_send()
        swap(at).wait_send()
    for ch in range(CHUNKS):
        landed(sb.at[ch], f_s.at[ch])
        landed(sg.at[ch], b_s.at[ch])


def local(table, projection_weight, output_weight, offsets, events, cotangent):
    vmem, anym = pl.BlockSpec(memory_space=pltpu.VMEM), pl.BlockSpec(memory_space=pl.ANY)
    dma = pltpu.SemaphoreType.DMA
    out, grad = pl.pallas_call(
        kernel,
        out_shape=(
            jax.ShapeDtypeStruct((EVENTS, WIDTH), BF16),
            jax.ShapeDtypeStruct((ROWS, WIDTH), F32),
        ),
        in_specs=[anym, vmem, vmem] + [anym] * 3,
        out_specs=(vmem, vmem),
        scratch_shapes=[
            pltpu.VMEM((ROWS, WIDTH), F32),
            pltpu.VMEM((WIDTH, 4 * WIDTH), BF16),
            pltpu.VMEM((WIDTH, WIDTH), BF16),
            pltpu.VMEM((EVENTS, WIDTH), BF16),
            dma((4,)),
            pltpu.VMEM((GROUPS, 2, ROWS, WIDTH), BF16),
            pltpu.VMEM((CHIPS, 1, 128), F32),
            pltpu.VMEM((CHIPS, 1, 128), F32),
            pltpu.VMEM((CHUNKS, CHIPS, 2 * MSG, SIDE), BF16),
            pltpu.VMEM((CHUNKS, CHIPS, 2 * MSG, SIDE), BF16),
            pltpu.VMEM((CHUNKS, CHIPS, 2 * MSG, SIDE), BF16),
            pltpu.VMEM((CHUNKS, CHIPS, 2 * MSG, SIDE), BF16),
            pltpu.VMEM((GROUPS, ROWS, WIDTH), F32),
            pltpu.VMEM((GROUPS, ROWS, WIDTH), BF16),
            pltpu.VMEM((GROUPS, ROWS, WIDTH), BF16),
            pltpu.VMEM((2, 6, ROWS, WIDTH), BF16),
            pltpu.VMEM((2, 6, ROWS, WIDTH), BF16),
            pltpu.VMEM((EVENTS, WIDTH), F32),
            pltpu.VMEM((4, EVENTS, WIDTH), F32),
            pltpu.VMEM((4, EVENTS, WIDTH), BF16),
            pltpu.VMEM((4, EVENTS, WIDTH), BF16),
            pltpu.VMEM((EVENTS, WIDTH), F32),
            dma((2, 6, 2)), dma((2, 6, 2)), dma((GROUPS, 2)), dma((GROUPS, 2)),
            dma, dma, dma((CHUNKS,)), dma((CHUNKS,)), dma((CHUNKS,)), dma((CHUNKS,)),
            dma((GROUPS,)), dma((GROUPS,)), dma((2, 6, 2)), dma((2, 6, 2)),
        ],
        compiler_params=pltpu.CompilerParams(
            collective_id=0, has_side_effects=True, vmem_limit_bytes=60 << 20
        ),
    )(
        table,
        offsets[0].T,
        events,
        cotangent.reshape(EVENTS, WIDTH),
        projection_weight,
        output_weight,
    )
    return out.reshape(cotangent.shape), grad


def solution(mesh):
    placed = (
        P(("grp", "loc"), None),
        P(),
        P(),
        P(("grp", "loc"), None, None),
        P(("grp", "loc"), None),
        P(("grp", "loc"), None, None),
    )
    return jax.shard_map(
        local,
        mesh=mesh,
        in_specs=placed,
        out_specs=(P(("grp", "loc"), None, None), P(("grp", "loc"), None)),
        check_vma=False,
    )
```
